512 devices in a mesh: row: 16 (over x, y_lo, core), col: 32 (over y_hi, z).
Axes of the slice: x: 4, y: 4 (y_hi: 2, y_lo: 2; y = y_hi * 2 + y_lo), z: 16, core: 2. Of those that a mesh axis runs over, the one named last changes fastest.
Arguments:
- interactions: bfloat16 [4096, 8192], P('col', 'row'), may hold values from -1 to 1
- regular: float32 [4096], P('col'), may hold values from 0.2 to 2
Outputs:
- factored: float32 [4, 1024, 4096], P(None, 'row', 'col')
The draws below stay inside these ranges and needn't reach their ends.
All inputs are finite; a program needn't handle non-finite values.
Results may differ from the reference program's by a relative error of at most 0.0003.
Values may be sent and summed in bfloat16 or wider, within the bound.
A program may use at most 128 MiB of HBM per device.

```python
import math
import jax
import jax.numpy as jnp
from jax import lax

PANEL = 1024
SPAN = 4
NI = 4096
USERS = 8192


def draw_interactions(key, part):
    key = jax.random.fold_in(key, 7)
    subkeys = jax.random.split(key, 4)
    cluster = jax.random.randint(subkeys[0], (NI,), 0, 64)
    loading = jax.random.truncated_normal(subkeys[1], -2.5, 2.5, (NI,), jnp.float32)
    profile = jax.random.truncated_normal(subkeys[2], -2.5, 2.5, (64, USERS), jnp.float32)
    noise_part = jax.random.truncated_normal(subkeys[3], -3.5, 3.5, (NI, USERS), jnp.float32)
    strength = 0.7
    shared = profile[cluster]
    values = (noise_part + strength * loading[:, None] * shared) / math.sqrt(USERS)
    return jnp.clip(values, -1.0, 1.0).astype(jnp.bfloat16)


def level_of(rng, dims, cuts, low, largest):
    def one(axis_at, shards_of):
        heights = jax.random.uniform(jax.random.fold_in(jax.random.fold_in(rng, 6), axis_at), (shards_of,), jnp.float32, low / len(cuts), largest / len(cuts))
        return jnp.repeat(jnp.exp(heights), dims[axis_at] // shards_of).reshape((-1,) + (1,) * (len(dims) - axis_at - 1))

    gain = one(*cuts[0])
    for cut in cuts[1:]:
        gain = gain * one(*cut)
    return gain


def setup_inputs(seed: int = 0) -> dict:
    seeds = jax.random.split(jax.random.key(seed), 3)
    interactions = draw_interactions(jax.random.fold_in(seeds[2], 71), 0)
    regular = jnp.clip(jnp.exp(math.log(2.0) - 2.3025851 * jax.random.uniform(seeds[1], (NI,), jnp.float32) ** level_of(seeds[1], (NI,), ((0, 32),), -0.2, 0.2)), 0.2, 2.0)
    return dict(interactions=interactions, regular=regular)


def reference(interactions, regular):
    gram_matrix = jnp.dot(interactions.astype(jnp.float32), interactions.T.astype(jnp.float32), preferred_element_type=jnp.float32)
    matrix = gram_matrix + jnp.diag(regular)
    lower_factor = jnp.linalg.cholesky(matrix[:PANEL, :PANEL])
    inverse = lax.linalg.triangular_solve(lower_factor, jnp.eye(PANEL, dtype=jnp.float32), left_side=True, lower=True)
    left_panel = jnp.dot(matrix[PANEL:, :PANEL], inverse.T, precision=lax.Precision.HIGHEST)
    trailing = matrix[PANEL:, PANEL:] - jnp.dot(left_panel, left_panel.T, precision=lax.Precision.HIGHEST)
    top_rows = jnp.concatenate([lower_factor, jnp.zeros((PANEL, NI - PANEL), jnp.float32)], 1)
    bottom = jnp.concatenate([left_panel, trailing], 1)
    return jnp.concatenate([top_rows, bottom], 0).reshape(SPAN, PANEL, NI)
```

```python
import functools
import jax
import jax.numpy as jnp
from jax import lax
from jax.experimental import pallas as pl
from jax.experimental.pallas import tpu as pltpu
from jax.sharding import PartitionSpec as P

PANEL = 1024
SPAN = 4
HI = lax.Precision.HIGHEST


def bl(x, lane):
    return jnp.broadcast_to(x[:, lane:lane+1], (8, 128))
def bs(x, row):
    return jnp.broadcast_to(x[row:row+1, :], (8, 128))

def factor(S, E):
    sub = lax.broadcasted_iota(jnp.int32, (8, 128), 0)
    U, V = [], []
    n = len(S)
    S = list(S); E = list(E)
    for b in range(n):
        C = [bl(S[b], 8*b+i) for i in range(8)]
        s = {}
        for i in range(8):
            for t in range(i, 8):
                s[t, i] = bs(C[i], t)
        R = [bs(S[b], i) for i in range(8)]
        Q = [bs(E[b], i) for i in range(8)]
        rd, l = [], {}
        for i in range(8):
            rd.append(1.0 / s[i, i])
            for t in range(i+1, 8):
                l[t, i] = s[t, i] * rd[i]
            for u in range(i+1, 8):
                for t in range(u, 8):
                    s[t, u] = s[t, u] - l[t, i] * s[u, i]
            for t in range(i+1, 8):
                R[t] = R[t] - l[t, i] * R[i]
                Q[t] = Q[t] - l[t, i] * Q[i]
        ru = [lax.rsqrt(s[i, i]) for i in range(8)]
        Uo = R[0] * ru[0]; Vo = Q[0] * ru[0]
        for i in range(1, 8):
            Uo = jnp.where(sub == i, R[i] * ru[i], Uo)
            Vo = jnp.where(sub == i, Q[i] * ru[i], Vo)
        U.append(Uo); V.append(Vo)
        if b == n-1: break
        Z = [None]*8; Y = [None]*8
        for i in range(7, -1, -1):
            z = R[i] * rd[i]; y = Q[i] * rd[i]
            for t in range(7, i, -1):
                z = z - l[t, i] * Z[t]
                y = y - l[t, i] * Y[t]
            Z[i] = z; Y[i] = y
        for g in range(b+1, n):
            c = [bl(S[g], 8*b+i) for i in range(8)]
            a0 = c[0]*Z[0]; a1 = c[1]*Z[1]; e0 = c[0]*Y[0]; e1 = c[1]*Y[1]
            for i in range(2, 8, 2):
                a0 = a0 + c[i]*Z[i]; a1 = a1 + c[i+1]*Z[i+1]
                e0 = e0 + c[i]*Y[i]; e1 = e1 + c[i+1]*Y[i+1]
            S[g] = S[g] - (a0 + a1)
            E[g] = E[g] - (e0 + e1)
    return U, V

def dt(a, b):
    return lax.dot_general(a, b, (((1,), (1,)), ((), ())), precision=HI, preferred_element_type=jnp.float32)

def k2(r, c, m_ref, tile_ref, out_ref, L, B, T, *, look):
    lane = lax.broadcasted_iota(jnp.int32, (8, 128), 1)
    sub = lax.broadcasted_iota(jnp.int32, (8, 128), 0)
    E0 = [jnp.where(lane == sub + 8*g, 1.0, 0.0).astype(jnp.float32) for g in range(16)]
    R = m_ref.shape[0]
    B[...] = m_ref[:, :128]
    for J in range(8):
        j0 = 128*J; r0 = j0 + 128
        S = [B[pl.ds(j0 + 8*g, 8), :] for g in range(16)]
        U, V = factor(S, E0)
        if J < 7 and look:
            if J == 0:
                T[pl.ds(r0, R-r0), :] = m_ref[pl.ds(r0, R-r0), pl.ds(r0, 128)]
            else:
                T[pl.ds(r0, R-r0), :] = m_ref[pl.ds(r0, R-r0), pl.ds(r0, 128)] - dt(L[pl.ds(r0, R-r0), pl.ds(0, j0)], L[pl.ds(r0, 128), pl.ds(0, j0)])
        Um = jnp.concatenate([jnp.where(lane >= sub + 8*g, U[g], 0.0) for g in range(16)], 0)
        Vm = jnp.concatenate(V, 0)
        L[pl.ds(j0, 128), pl.ds(j0, 128)] = Um.T
        if look:
            Pn = dt(B[pl.ds(r0, 128), :], Vm)
            L[pl.ds(r0, 128), pl.ds(j0, 128)] = Pn
            if J < 7:
                Bn = T[pl.ds(r0, 128), :] - dt(Pn, Pn)
                r1 = r0 + 128
                Pr = dt(B[pl.ds(r1, R-r1), :], Vm)
                L[pl.ds(r1, R-r1), pl.ds(j0, 128)] = Pr
                B[pl.ds(r0, 128), :] = Bn
                B[pl.ds(r1, R-r1), :] = T[pl.ds(r1, R-r1), :] - dt(Pr, Pn)
            else:
                r1 = r0 + 128
                L[pl.ds(r1, R-r1), pl.ds(j0, 128)] = dt(B[pl.ds(r1, R-r1), :], Vm)
        else:
            L[pl.ds(r0, R-r0), pl.ds(j0, 128)] = dt(B[pl.ds(r0, R-r0), :], Vm)
            if J < 7:
                B[pl.ds(r0, R-r0), :] = m_ref[pl.ds(r0, R-r0), pl.ds(r0, 128)] - dt(L[pl.ds(r0, R-r0), pl.ds(0, r0)], L[pl.ds(r0, 128), pl.ds(0, r0)])
    for J in range(7):
        L[pl.ds(128*J, 128), pl.ds(128*(J+1), 128*(7-J))] = jnp.zeros((128, 128*(7-J)), jnp.float32)
    tr = tile_ref[1:].reshape(192, 128) - dt(L[pl.ds(1024, 192), :], L[pl.ds(1216, 128), :])
    cc = jnp.minimum(c, 7)
    col = pl.multiple_of(cc*128, 128)
    first = L[pl.ds(pl.multiple_of(r*64, 64), 64), pl.ds(col, 128)]
    lt = L[pl.ds(1024, 192), pl.ds(col, 128)]
    inp = c < 8
    out_ref[0] = jnp.where(inp, first, 0.0)
    out_ref[1:] = jnp.where(inp, lt, tr).reshape(3, 64, 128)


def finish_kernel(m_ref, tile_ref, out_ref, L, B, T):
    k2(lax.axis_index("row"), lax.axis_index("col"), m_ref, tile_ref, out_ref, L, B, T, look=True)


def finish(m, tile):
    rows = m.shape[0]
    return pl.pallas_call(
        finish_kernel,
        out_shape=jax.ShapeDtypeStruct(tile.shape, jnp.float32),
        scratch_shapes=[
            pltpu.VMEM((rows, PANEL), jnp.float32),
            pltpu.VMEM((rows, 128), jnp.float32),
            pltpu.VMEM((rows, 128), jnp.float32),
        ],
        compiler_params=pltpu.CompilerParams(vmem_limit_bytes=50 * 1024 * 1024),
        name="finish",
    )(m, tile)


def body(interactions, regular):
    row_count = lax.axis_size("row")
    row_index = lax.axis_index("row")
    col_index = lax.axis_index("col")
    block_width = interactions.shape[0]
    user_count = interactions.shape[1]
    band_rows = PANEL // row_count
    per_owner = SPAN * band_rows
    everyone = lax.all_gather(interactions, "col", axis=0, tiled=True)
    grouped = everyone.reshape(SPAN, row_count, band_rows, user_count)
    term_block = jnp.einsum(
        "kotu,ju->oktj", grouped, interactions, preferred_element_type=jnp.float32
    )
    grid_tile = lax.psum_scatter(
        term_block.reshape(per_owner * row_count, block_width),
        "row",
        scatter_dimension=0,
        tiled=True,
    ).reshape(SPAN, band_rows, block_width)
    row_items = (
        jnp.arange(SPAN, dtype=jnp.int32)[:, None] * PANEL
        + row_index * band_rows
        + jnp.arange(band_rows, dtype=jnp.int32)[None, :]
    )
    col_items = col_index * block_width + jnp.arange(block_width, dtype=jnp.int32)
    on_diagonal = row_items[:, :, None] == col_items[None, None, :]
    grid_tile = grid_tile + jnp.where(on_diagonal, regular[None, None, :], jnp.float32(0.0))
    row_band = lax.all_gather(grid_tile, "col", axis=2, tiled=True)[:, :, :PANEL]
    diagonal = lax.all_gather(row_band[0], "row", axis=0, tiled=True)
    mcols = lax.all_gather(grid_tile[0], "row", axis=0, tiled=True).T
    m = jnp.concatenate([diagonal, row_band[1:].reshape(3 * band_rows, PANEL), mcols], 0)
    return finish(m, grid_tile)


def solution(mesh):
    return jax.shard_map(
        body,
        mesh=mesh,
        in_specs=(P("col", "row"), P("col")),
        out_specs=P(None, "row", "col"),
        check_vma=False,
    )
```

```python
import jax
import jax.numpy as jnp
from jax import lax
from jax.experimental import pallas as pl
from jax.experimental.pallas import tpu as pltpu
from jax.sharding import PartitionSpec as P

PANEL = 1024
RING = 16
HI = lax.Precision.HIGHEST
MESH = pl.DeviceIdType.MESH


def gather_kernel(x_ref, reg_ref, tile_ref, band_ref, xg, wc, prod, parts, halves,
                  ring_send, ring_recv, pair_send, pair_recv, part_send, part_recv, panel_send, panel_recv):
    r = lax.axis_index("row")
    c = lax.axis_index("col")
    h = c // RING
    z = c % RING
    other = 1 - h
    chip = r // 2
    core = r % 2
    right = h * RING + (z + 1) % RING
    left = h * RING + (z + RING - 1) % RING
    partner = other * RING + z

    barrier = pltpu.get_barrier_semaphore()
    for near in (left, right, partner):
        pl.semaphore_signal(barrier, inc=1, device_id=(r, near), device_id_type=MESH)
    for step in range(1, 16):
        pl.semaphore_signal(barrier, inc=1, device_id=((r + step) % 16, c), device_id_type=MESH)
    pl.semaphore_wait(barrier, 18)

    def remote(src, dst, send, recv, device):
        return pltpu.make_async_remote_copy(
            src_ref=src, dst_ref=dst, send_sem=send, recv_sem=recv, device_id=device, device_id_type=MESH
        )

    swap = remote(x_ref, wc.at[h], pair_send.at[0], pair_recv.at[0], (r, partner))
    swap.start()

    def ring_copy(way, step, half):
        owner = (z - step + 1 + RING) % RING if way == 0 else (z + step - 1) % RING
        rows = pl.ds(64 * half, 64)
        src = x_ref.at[rows] if step == 1 else xg.at[owner, rows]
        return remote(src, xg.at[owner, rows], ring_send.at[way, step - 1, half],
                      ring_recv.at[way, step - 1, half], (r, right if way == 0 else left))

    steps = (8, 7)
    for half in range(2):
        for way in range(2):
            ring_copy(way, 1, half).start()
    wc[h] = x_ref[...]

    def multiply(owner, block):
        both = wc[...].reshape(256, 512)
        product = lax.dot_general(block, both, (((1,), (1,)), ((), ())), preferred_element_type=jnp.float32)
        prod[owner] = product.reshape(2, 64, 256)
        place = owner % 8
        half_k = owner // 8
        for to in range(2):
            mine = jnp.logical_and(place == chip, core == to)

            @pl.when(jnp.logical_not(mine))
            def _():
                remote(prod.at[owner, to], parts.at[half_k, r], part_send, part_recv.at[half_k],
                       (2 * place + to, c)).start()

            @pl.when(mine)
            def _():
                parts[half_k, r] = prod[owner, to]

    swap.wait()
    multiply(z, x_ref[...])
    for step in range(1, 9):
        for half in range(2):
            for way in range(2):
                if step <= steps[way]:
                    ring_copy(way, step, half).wait_recv()
                    if step < steps[way]:
                        ring_copy(way, step + 1, half).start()
        for way in range(2):
            if step <= steps[way]:
                owner = (z - step + RING) % RING if way == 0 else (z + step) % RING
                multiply(owner, xg[owner])

    lane = lax.broadcasted_iota(jnp.int32, (64, 128), 1)
    sub = lax.broadcasted_iota(jnp.int32, (64, 128), 0)
    for half_k in range(2):
        pltpu.make_async_copy(parts.at[half_k, pl.ds(0, 15)], parts.at[half_k, pl.ds(0, 15)], part_recv.at[half_k]).wait()
        total = parts[half_k, 0]
        for source in range(1, 16):
            total = total + parts[half_k, source]
        for side in range(2):
            block = total[:, 128 * side:128 * side + 128]
            hit = jnp.logical_and(chip + 8 * half_k == z, h == side)
            diagonal = jnp.logical_and(lane == sub + 64 * core, hit)
            halves[side, half_k] = block + jnp.where(diagonal, jnp.broadcast_to(reg_ref[...], (64, 128)), 0.0)

    give = remote(halves.at[other], tile_ref.at[pl.ds(2 * h, 2)], pair_send.at[1], pair_recv.at[1], (r, partner))
    give.start()
    tile_ref[pl.ds(2 * h, 2)] = halves[h]
    in_panel = z < 8
    lend = remote(halves.at[0], band_ref.at[jnp.minimum(z, 7), pl.ds(0, 2)], pair_send.at[2], pair_recv.at[2], (r, partner))

    @pl.when(jnp.logical_and(in_panel, h == 0))
    def _():
        lend.start()

    @pl.when(jnp.logical_and(in_panel, h == 1))
    def _():
        band_ref[z, pl.ds(2, 2)] = halves[0]
        lend.wait_recv()

    give.wait()

    @pl.when(jnp.logical_and(in_panel, h == 0))
    def _():
        band_ref[z] = tile_ref[...]
        lend.wait_send()

    def panel_copy(way, step):
        owner = (z - step + 1 + RING) % RING if way == 0 else (z + step - 1) % RING
        slot = jnp.minimum(owner, 7)
        return owner < 8, remote(band_ref.at[slot], band_ref.at[slot], panel_send.at[way, step - 1],
                                 panel_recv.at[way, step - 1], (r, right if way == 0 else left))

    def panel_arrival(way, step):
        owner = (z - step + RING) % RING if way == 0 else (z + step) % RING
        slot = jnp.minimum(owner, 7)
        return owner < 8, remote(band_ref.at[slot], band_ref.at[slot], panel_send.at[way, step - 1],
                                 panel_recv.at[way, step - 1], (r, right if way == 0 else left))

    for step in range(1, 9):
        for way in range(2):
            if step <= steps[way]:
                if step > 1:
                    here, copy = panel_arrival(way, step - 1)
                    pl.when(here)(copy.wait_recv)
                here, copy = panel_copy(way, step)
                pl.when(here)(copy.start)
    for way in range(2):
        here, copy = panel_arrival(way, steps[way])
        pl.when(here)(copy.wait_recv)
    for way in range(2):
        for step in range(1, steps[way] + 1):
            here, copy = panel_copy(way, step)
            pl.when(here)(copy.wait_send)
            for half in range(2):
                ring_copy(way, step, half).wait_send()
    pltpu.make_async_copy(prod.at[pl.ds(0, 15)], prod.at[pl.ds(0, 15)], part_send).wait()


def gather(interactions, regular):
    vmem = pl.BlockSpec(memory_space=pltpu.VMEM)
    return pl.pallas_call(
        gather_kernel,
        out_shape=[
            jax.ShapeDtypeStruct((4, 64, 128), jnp.float32),
            jax.ShapeDtypeStruct((8, 4, 64, 128), jnp.float32),
        ],
        in_specs=[vmem, vmem],
        out_specs=[vmem, vmem],
        scratch_shapes=[
            pltpu.VMEM((RING, 128, 512), jnp.bfloat16),
            pltpu.VMEM((2, 128, 512), jnp.bfloat16),
            pltpu.VMEM((RING, 2, 64, 256), jnp.float32),
            pltpu.VMEM((2, 16, 64, 256), jnp.float32),
            pltpu.VMEM((2, 2, 64, 128), jnp.float32),
            pltpu.SemaphoreType.DMA((2, 8, 2)),
            pltpu.SemaphoreType.DMA((2, 8, 2)),
            pltpu.SemaphoreType.DMA((3,)),
            pltpu.SemaphoreType.DMA((3,)),
            pltpu.SemaphoreType.DMA,
            pltpu.SemaphoreType.DMA((2,)),
            pltpu.SemaphoreType.DMA((2, 8)),
            pltpu.SemaphoreType.DMA((2, 8)),
        ],
        compiler_params=pltpu.CompilerParams(
            collective_id=0, has_side_effects=True, vmem_limit_bytes=50 * 1024 * 1024
        ),
        name="gather",
    )(interactions, regular.reshape(1, 128))


def bl(x, lane):
    return jnp.broadcast_to(x[:, lane:lane+1], (8, 128))
def bs(x, row):
    return jnp.broadcast_to(x[row:row+1, :], (8, 128))

def factor(S, E):
    sub = lax.broadcasted_iota(jnp.int32, (8, 128), 0)
    U, V = [], []
    n = len(S)
    S = list(S); E = list(E)
    for b in range(n):
        C = [bl(S[b], 8*b+i) for i in range(8)]
        s = {}
        for i in range(8):
            for t in range(i, 8):
                s[t, i] = bs(C[i], t)
        R = [bs(S[b], i) for i in range(8)]
        Q = [bs(E[b], i) for i in range(8)]
        rd, l = [], {}
        for i in range(8):
            rd.append(1.0 / s[i, i])
            for t in range(i+1, 8):
                l[t, i] = s[t, i] * rd[i]
            for u in range(i+1, 8):
                for t in range(u, 8):
                    s[t, u] = s[t, u] - l[t, i] * s[u, i]
            for t in range(i+1, 8):
                R[t] = R[t] - l[t, i] * R[i]
                Q[t] = Q[t] - l[t, i] * Q[i]
        ru = [lax.rsqrt(s[i, i]) for i in range(8)]
        Uo = R[0] * ru[0]; Vo = Q[0] * ru[0]
        for i in range(1, 8):
            Uo = jnp.where(sub == i, R[i] * ru[i], Uo)
            Vo = jnp.where(sub == i, Q[i] * ru[i], Vo)
        U.append(Uo); V.append(Vo)
        if b == n-1: break
        Z = [None]*8; Y = [None]*8
        for i in range(7, -1, -1):
            z = R[i] * rd[i]; y = Q[i] * rd[i]
            for t in range(7, i, -1):
                z = z - l[t, i] * Z[t]
                y = y - l[t, i] * Y[t]
            Z[i] = z; Y[i] = y
        for g in range(b+1, n):
            c = [bl(S[g], 8*b+i) for i in range(8)]
            a0 = c[0]*Z[0]; a1 = c[1]*Z[1]; e0 = c[0]*Y[0]; e1 = c[1]*Y[1]
            for i in range(2, 8, 2):
                a0 = a0 + c[i]*Z[i]; a1 = a1 + c[i+1]*Z[i+1]
                e0 = e0 + c[i]*Y[i]; e1 = e1 + c[i+1]*Y[i+1]
            S[g] = S[g] - (a0 + a1)
            E[g] = E[g] - (e0 + e1)
    return U, V


def dt(a, b):
    return lax.dot_general(a, b, (((1,), (1,)), ((), ())), precision=HI, preferred_element_type=jnp.float32)


def finish_kernel(m_ref, band_ref, tile_ref, out_ref, L, B, T):
    r = lax.axis_index("row")
    c = lax.axis_index("col")
    lane = lax.broadcasted_iota(jnp.int32, (8, 128), 1)
    sub = lax.broadcasted_iota(jnp.int32, (8, 128), 0)
    E0 = [jnp.where(lane == sub + 8 * g, 1.0, 0.0).astype(jnp.float32) for g in range(16)]
    R = L.shape[0]

    def pieces(J):
        above = 2 * J
        yield 128 * J, 1024 - 128 * J, m_ref[above:, J].reshape(1024 - 128 * J, 128)
        yield 1024, 192, band_ref[J, 1:].reshape(192, 128)
        yield 1216, 128, m_ref[above:above + 2, 8].reshape(128, 128).T

    for at, count, value in pieces(0):
        B[pl.ds(at, count), :] = value
    for J in range(8):
        j0 = 128 * J
        r0 = j0 + 128
        r1 = r0 + 128
        S = [B[pl.ds(j0 + 8 * g, 8), :] for g in range(16)]
        U, V = factor(S, E0)
        if J < 7:
            for at, count, value in pieces(J + 1):
                if J > 0:
                    value = value - dt(L[pl.ds(at, count), pl.ds(0, j0)], L[pl.ds(r0, 128), pl.ds(0, j0)])
                T[pl.ds(at, count), :] = value
        Um = jnp.concatenate([jnp.where(lane >= sub + 8 * g, U[g], 0.0) for g in range(16)], 0)
        Vm = jnp.concatenate(V, 0)
        L[pl.ds(j0, 128), pl.ds(j0, 128)] = Um.T
        if J < 7:
            Pn = dt(B[pl.ds(r0, 128), :], Vm)
            L[pl.ds(r0, 128), pl.ds(j0, 128)] = Pn
            Bn = T[pl.ds(r0, 128), :] - dt(Pn, Pn)
            Pr = dt(B[pl.ds(r1, R - r1), :], Vm)
            L[pl.ds(r1, R - r1), pl.ds(j0, 128)] = Pr
            B[pl.ds(r0, 128), :] = Bn
            B[pl.ds(r1, R - r1), :] = T[pl.ds(r1, R - r1), :] - dt(Pr, Pn)
        else:
            L[pl.ds(r0, R - r0), pl.ds(j0, 128)] = dt(B[pl.ds(r0, R - r0), :], Vm)
    for J in range(7):
        L[pl.ds(128 * J, 128), pl.ds(128 * (J + 1), 128 * (7 - J))] = jnp.zeros((128, 128 * (7 - J)), jnp.float32)
    tr = tile_ref[1:].reshape(192, 128) - dt(L[pl.ds(1024, 192), :], L[pl.ds(1216, 128), :])
    column = pl.multiple_of(jnp.minimum(c, 7) * 128, 128)
    first = L[pl.ds(pl.multiple_of(r * 64, 64), 64), pl.ds(column, 128)]
    solved = L[pl.ds(1024, 192), pl.ds(column, 128)]
    in_panel = c < 8
    out_ref[0] = jnp.where(in_panel, first, 0.0)
    out_ref[1:] = jnp.where(in_panel, solved, tr).reshape(3, 64, 128)


def finish(m, band, tile):
    rows = 1024 + 192 + 128
    return pl.pallas_call(
        finish_kernel,
        out_shape=jax.ShapeDtypeStruct(tile.shape, jnp.float32),
        scratch_shapes=[
            pltpu.VMEM((rows, PANEL), jnp.float32),
            pltpu.VMEM((rows, 128), jnp.float32),
            pltpu.VMEM((rows, 128), jnp.float32),
        ],
        compiler_params=pltpu.CompilerParams(vmem_limit_bytes=50 * 1024 * 1024),
        name="finish",
    )(m, band, tile)


def body(interactions, regular):
    tile, band = gather(interactions, regular)
    mine = jnp.concatenate([band[:, 0], tile[:1]], 0)
    m = lax.all_gather(mine, "row", axis=0)
    return finish(m, band, tile)


def solution(mesh):
    return jax.shard_map(
        body,
        mesh=mesh,
        in_specs=(P("col", "row"), P("col")),
        out_specs=P(None, "row", "col"),
        check_vma=False,
    )
```

```python
import jax
import jax.numpy as jnp
from jax import lax
from jax.experimental import pallas as pl
from jax.experimental.pallas import tpu as pltpu
from jax.sharding import PartitionSpec as P

PANEL = 1024
RING = 16
CHUNKS = 2
GROUPS = ((0, 2, 0), (2, 1, 0), (3, 2, 4), (5, 4, 8))
HI = lax.Precision.HIGHEST
MESH = pl.DeviceIdType.MESH


def bl(x, lane):
    return jnp.broadcast_to(x[:, lane:lane+1], (8, 128))
def bs(x, row):
    return jnp.broadcast_to(x[row:row+1, :], (8, 128))

def factor(S, E):
    sub = lax.broadcasted_iota(jnp.int32, (8, 128), 0)
    U, V = [], []
    n = len(S)
    S = list(S); E = list(E)
    for b in range(n):
        C = [bl(S[b], 8*b+i) for i in range(8)]
        s = {}
        for i in range(8):
            for t in range(i, 8):
                s[t, i] = bs(C[i], t)
        R = [bs(S[b], i) for i in range(8)]
        Q = [bs(E[b], i) for i in range(8)]
        rd, l = [], {}
        for i in range(8):
            rd.append(1.0 / s[i, i])
            for t in range(i+1, 8):
                l[t, i] = s[t, i] * rd[i]
            for u in range(i+1, 8):
                for t in range(u, 8):
                    s[t, u] = s[t, u] - l[t, i] * s[u, i]
            for t in range(i+1, 8):
                R[t] = R[t] - l[t, i] * R[i]
                Q[t] = Q[t] - l[t, i] * Q[i]
        ru = [lax.rsqrt(s[i, i]) for i in range(8)]
        Uo = R[0] * ru[0]; Vo = Q[0] * ru[0]
        for i in range(1, 8):
            Uo = jnp.where(sub == i, R[i] * ru[i], Uo)
            Vo = jnp.where(sub == i, Q[i] * ru[i], Vo)
        U.append(Uo); V.append(Vo)
        if b == n-1: break
        Z = [None]*8; Y = [None]*8
        for i in range(7, -1, -1):
            z = R[i] * rd[i]; y = Q[i] * rd[i]
            for t in range(7, i, -1):
                z = z - l[t, i] * Z[t]
                y = y - l[t, i] * Y[t]
            Z[i] = z; Y[i] = y
        for g in range(b+1, n):
            c = [bl(S[g], 8*b+i) for i in range(8)]
            a0 = c[0]*Z[0]; a1 = c[1]*Z[1]; e0 = c[0]*Y[0]; e1 = c[1]*Y[1]
            for i in range(2, 8, 2):
                a0 = a0 + c[i]*Z[i]; a1 = a1 + c[i+1]*Z[i+1]
                e0 = e0 + c[i]*Y[i]; e1 = e1 + c[i+1]*Y[i+1]
            S[g] = S[g] - (a0 + a1)
            E[g] = E[g] - (e0 + e1)
    return U, V


def dt(a, b):
    return lax.dot_general(a, b, (((1,), (1,)), ((), ())), precision=HI, preferred_element_type=jnp.float32)


def whole_kernel(x_ref, reg_ref, out_ref, tile_ref, m_ref, band_ref, L, B, T, xg, wc, wt, prod, parts, halves,
                 ring_send, ring_recv, pair_send, pair_recv, part_send, part_recv, hub_send, hub_recv,
                 near_send, near_recv, row_send, row_recv):
    r = lax.axis_index("row")
    c = lax.axis_index("col")
    h = c // RING
    z = c % RING
    q = z % 8
    other = 1 - h
    chip = r // 2
    core = r % 2
    partner = other * RING + z

    def along(distance):
        return h * RING + (z + distance + RING) % RING

    right, left = along(1), along(-1)
    hubs = (partner, along(8), other * RING + (z + 8) % RING)
    near = (1, -1, 2, -2, 3, -3, 4)

    barrier = pltpu.get_barrier_semaphore()
    for place in hubs + tuple(along(d) for d in near) + (along(-4),):
        pl.semaphore_signal(barrier, inc=1, device_id=(r, place), device_id_type=MESH)
    for step in range(1, 16):
        pl.semaphore_signal(barrier, inc=1, device_id=((r + step) % 16, c), device_id_type=MESH)
    pl.semaphore_wait(barrier, 26)

    def remote(src, dst, send, recv, device):
        return pltpu.make_async_remote_copy(
            src_ref=src, dst_ref=dst, send_sem=send, recv_sem=recv, device_id=device, device_id_type=MESH
        )

    swap = remote(x_ref, wc.at[h], pair_send.at[0], pair_recv.at[0], (r, partner))

    def ring_copy(way, step, chunk):
        owner = (z - step + 1 + RING) % RING if way == 0 else (z + step - 1) % RING
        rows = pl.ds(128 // CHUNKS * chunk, 128 // CHUNKS)
        src = x_ref.at[rows] if step == 1 else xg.at[owner, rows]
        return remote(src, xg.at[owner, rows], ring_send.at[way, step - 1, chunk],
                      ring_recv.at[way, step - 1, chunk], (r, right if way == 0 else left))

    steps = (8, 7)
    for chunk in range(CHUNKS):
        for way in range(2):
            ring_copy(way, 1, chunk).start()
    swap.start()
    wc[h] = x_ref[...]

    def multiply(owner, block):
        product = jnp.dot(block, wt[...], preferred_element_type=jnp.float32)
        prod[owner] = product.reshape(2, 64, 256)
        place = owner % 8
        half_k = owner // 8
        for to in range(2):
            mine = jnp.logical_and(place == chip, core == to)

            @pl.when(jnp.logical_not(mine))
            def _():
                remote(prod.at[owner, to], parts.at[half_k, r], part_send, part_recv.at[half_k],
                       (2 * place + to, c)).start()

            @pl.when(mine)
            def _():
                parts[half_k, r] = prod[owner, to]

    for step in range(1, 9):
        for chunk in range(CHUNKS):
            for way in range(2):
                if step <= steps[way]:
                    ring_copy(way, step, chunk).wait_recv()
                    if step < steps[way]:
                        ring_copy(way, step + 1, chunk).start()
        if step == 1:
            swap.wait()
            wt[...] = wc[...].reshape(256, 512).T
            multiply(z, x_ref[...])
        for way in range(2):
            if step <= steps[way]:
                owner = (z - step + RING) % RING if way == 0 else (z + step) % RING
                multiply(owner, xg[owner])

    lane = lax.broadcasted_iota(jnp.int32, (64, 128), 1)
    sub = lax.broadcasted_iota(jnp.int32, (64, 128), 0)
    for half_k in range(2):
        pltpu.make_async_copy(parts.at[half_k, pl.ds(0, 15)], parts.at[half_k, pl.ds(0, 15)], part_recv.at[half_k]).wait()
        total = parts[half_k, 0]
        for source in range(1, 16):
            total = total + parts[half_k, source]
        for side in range(2):
            block = total[:, 128 * side:128 * side + 128]
            hit = jnp.logical_and(chip + 8 * half_k == z, h == side)
            diagonal = jnp.logical_and(lane == sub + 64 * core, hit)
            halves[side, half_k] = block + jnp.where(diagonal, jnp.broadcast_to(reg_ref[...], (64, 128)), 0.0)

    give = remote(halves.at[other], tile_ref.at[pl.ds(2 * h, 2)], pair_send.at[1], pair_recv.at[1], (r, partner))
    lead = [remote(halves.at[0, 0], m_ref.at[r, 1 + q], hub_send.at[0, i], hub_recv.at[0], (r, hubs[i])) for i in range(3)]
    second = [remote(halves.at[0, 1], band_ref.at[q, 0], hub_send.at[1, i], hub_recv.at[1], (r, hubs[i])) for i in range(3)]
    third = [remote(halves.at[0], band_ref.at[q, pl.ds(1, 2)], hub_send.at[2, i], hub_recv.at[2], (r, hubs[i])) for i in range(3)]
    source0 = jnp.logical_and(z < 8, h == 0)
    source1 = jnp.logical_and(z < 8, h == 1)

    @pl.when(source0)
    def _():
        for copy in lead + second:
            copy.start()
        m_ref[r, 1 + q] = halves[0, 0]
        band_ref[q, 0] = halves[0, 1]

    @pl.when(source1)
    def _():
        for copy in third:
            copy.start()
        band_ref[q, pl.ds(1, 2)] = halves[0]

    give.start()
    tile_ref[pl.ds(2 * h, 2)] = halves[h]

    @pl.when(jnp.logical_not(source0))
    def _():
        lead[0].wait_recv()

    near_copies = [remote(m_ref.at[r, 1 + q], m_ref.at[r, 1 + q], near_send.at[0, i], near_recv.at[0, i], (r, along(d)))
                   for i, d in enumerate(near)]
    band_copies = [remote(band_ref.at[q], band_ref.at[q], near_send.at[1, i], near_recv.at[1, i], (r, along(d)))
                   for i, d in enumerate(near)]
    for copy in near_copies:
        copy.start()

    @pl.when(jnp.logical_not(source0))
    def _():
        second[0].wait_recv()

    @pl.when(jnp.logical_not(source1))
    def _():
        third[0].wait_recv()

    give.wait()
    m_ref[r, 0] = tile_ref[0]
    for copy in near_copies:
        copy.wait_recv()

    def row_copy(group, step):
        at, count, _ = GROUPS[group]
        part = m_ref.at[r, pl.ds(at, count)]
        return remote(part, part, row_send.at[group, step - 1], row_recv.at[group], ((r + step) % 16, c))

    def row_wait(group):
        at, count, low = GROUPS[group]

        def arrive(sources):
            part = m_ref.at[pl.ds(0, sources), pl.ds(at, count)]
            pltpu.make_async_copy(part, part, row_recv.at[group]).wait()

        if low == 0:
            arrive(15)
        else:
            pl.when(r >= low)(lambda: arrive(15 - low))
            pl.when(r < low)(lambda: arrive(16 - low))

    def row_sends(group, act):
        def each():
            for step in range(1, 16):
                act(row_copy(group, step))

        if GROUPS[group][2] == 0:
            each()
        else:
            pl.when(r >= GROUPS[group][2])(each)

    for group in range(len(GROUPS)):
        row_sends(group, lambda copy: copy.start())
        if group == 0:
            for copy in band_copies:
                copy.start()
    row_wait(0)

    lane = lax.broadcasted_iota(jnp.int32, (8, 128), 1)
    sub = lax.broadcasted_iota(jnp.int32, (8, 128), 0)
    E0 = [jnp.where(lane == sub + 8 * g, 1.0, 0.0).astype(jnp.float32) for g in range(16)]
    R = L.shape[0]

    def pieces(J):
        above = 2 * J
        yield 128 * J, 1024 - 128 * J, m_ref[above:, 1 + J].reshape(1024 - 128 * J, 128)
        yield 1024, 192, band_ref[J].reshape(192, 128)
        yield 1216, 128, m_ref[above:above + 2, 0].reshape(128, 128).T

    B[pl.ds(0, 1024), :] = m_ref[:, 1].reshape(1024, 128)
    B[pl.ds(1216, 128), :] = m_ref[:2, 0].reshape(128, 128).T
    for J in range(8):
        j0 = 128 * J
        r0 = j0 + 128
        r1 = r0 + 128
        S = [B[pl.ds(j0 + 8 * g, 8), :] for g in range(16)]
        U, V = factor(S, E0)
        if J == 0:
            for copy in band_copies:
                copy.wait_recv()
            B[pl.ds(1024, 192), :] = band_ref[0].reshape(192, 128)
        for group in range(1, len(GROUPS)):
            if GROUPS[group][0] == J + 2:
                row_wait(group)
        if J < 7:
            for at, count, value in pieces(J + 1):
                if J > 0:
                    value = value - dt(L[pl.ds(at, count), pl.ds(0, j0)], L[pl.ds(r0, 128), pl.ds(0, j0)])
                T[pl.ds(at, count), :] = value
        Um = jnp.concatenate([jnp.where(lane >= sub + 8 * g, U[g], 0.0) for g in range(16)], 0)
        Vm = jnp.concatenate(V, 0)
        L[pl.ds(j0, 128), pl.ds(j0, 128)] = Um.T
        if J < 7:
            Pn = dt(B[pl.ds(r0, 128), :], Vm)
            L[pl.ds(r0, 128), pl.ds(j0, 128)] = Pn
            Bn = T[pl.ds(r0, 128), :] - dt(Pn, Pn)
            Pr = dt(B[pl.ds(r1, R - r1), :], Vm)
            L[pl.ds(r1, R - r1), pl.ds(j0, 128)] = Pr
            B[pl.ds(r0, 128), :] = Bn
            B[pl.ds(r1, R - r1), :] = T[pl.ds(r1, R - r1), :] - dt(Pr, Pn)
        else:
            L[pl.ds(r0, R - r0), pl.ds(j0, 128)] = dt(B[pl.ds(r0, R - r0), :], Vm)
    for J in range(7):
        L[pl.ds(128 * J, 128), pl.ds(128 * (J + 1), 128 * (7 - J))] = jnp.zeros((128, 128 * (7 - J)), jnp.float32)
    tr = tile_ref[1:].reshape(192, 128) - dt(L[pl.ds(1024, 192), :], L[pl.ds(1216, 128), :])
    column = pl.multiple_of(jnp.minimum(c, 7) * 128, 128)
    first = L[pl.ds(pl.multiple_of(r * 64, 64), 64), pl.ds(column, 128)]
    solved = L[pl.ds(1024, 192), pl.ds(column, 128)]
    in_panel = c < 8
    out_ref[0] = jnp.where(in_panel, first, 0.0)
    out_ref[1:] = jnp.where(in_panel, solved, tr).reshape(3, 64, 128)

    for group in range(len(GROUPS)):
        row_sends(group, lambda copy: copy.wait_send())
    for way in range(2):
        for step in range(1, steps[way] + 1):
            for chunk in range(CHUNKS):
                ring_copy(way, step, chunk).wait_send()
    for copy in near_copies + band_copies:
        copy.wait_send()

    @pl.when(source0)
    def _():
        for copy in lead + second:
            copy.wait_send()

    @pl.when(source1)
    def _():
        for copy in third:
            copy.wait_send()

    pltpu.make_async_copy(prod.at[pl.ds(0, 15)], prod.at[pl.ds(0, 15)], part_send).wait()


def body(interactions, regular):
    vmem = pl.BlockSpec(memory_space=pltpu.VMEM)
    dma = pltpu.SemaphoreType.DMA
    rows = 1024 + 192 + 128
    return pl.pallas_call(
        whole_kernel,
        out_shape=jax.ShapeDtypeStruct((4, 64, 128), jnp.float32),
        in_specs=[vmem, vmem],
        out_specs=vmem,
        scratch_shapes=[
            pltpu.VMEM((4, 64, 128), jnp.float32),
            pltpu.VMEM((16, 9, 64, 128), jnp.float32),
            pltpu.VMEM((8, 3, 64, 128), jnp.float32),
            pltpu.VMEM((rows, PANEL), jnp.float32),
            pltpu.VMEM((rows, 128), jnp.float32),
            pltpu.VMEM((rows, 128), jnp.float32),
            pltpu.VMEM((RING, 128, 512), jnp.bfloat16),
            pltpu.VMEM((2, 128, 512), jnp.bfloat16),
            pltpu.VMEM((512, 256), jnp.bfloat16),
            pltpu.VMEM((RING, 2, 64, 256), jnp.float32),
            pltpu.VMEM((2, 16, 64, 256), jnp.float32),
            pltpu.VMEM((2, 2, 64, 128), jnp.float32),
            dma((2, 8, CHUNKS)),
            dma((2, 8, CHUNKS)),
            dma((2,)),
            dma((2,)),
            dma,
            dma((2,)),
            dma((3, 3)),
            dma((3,)),
            dma((2, 7)),
            dma((2, 7)),
            dma((len(GROUPS), 15)),
            dma((len(GROUPS),)),
        ],
        compiler_params=pltpu.CompilerParams(
            collective_id=0, has_side_effects=True, vmem_limit_bytes=50 * 1024 * 1024
        ),
        name="whole",
    )(interactions, regular.reshape(1, 128))


def solution(mesh):
    return jax.shard_map(
        body,
        mesh=mesh,
        in_specs=(P("col", "row"), P("col")),
        out_specs=P(None, "row", "col"),
        check_vma=False,
    )
```

```python
import jax
import jax.numpy as jnp
from jax import lax
from jax.experimental import pallas as pl
from jax.experimental.pallas import tpu as pltpu
from jax.sharding import PartitionSpec as P

PANEL = 1024
RING = 16
CHUNKS = 2
GROUPS = ((0, 1, 1), (1, 1, 1), (2, 2, 2), (4, 4, 4), (8, 1, 0))
OWN = 4
FURTHER = ((), (), (), (0, 1), (2, 3), (4,), (5,), (6,))
HI = lax.Precision.HIGHEST
MESH = pl.DeviceIdType.MESH


def bl(x, lane):
    return jnp.broadcast_to(x[:, lane:lane+1], (8, 128))
def bs(x, row):
    return jnp.broadcast_to(x[row:row+1, :], (8, 128))

def factor(S, E, scr, middle):
    sub = lax.broadcasted_iota(jnp.int32, (8, 128), 0)
    U, V = [], []
    n = len(S)
    S = list(S); E = list(E)
    for b in range(n):
        if b == n // 2:
            middle()
        C = [bl(S[b], 8*b+i) for i in range(8)]
        s = {}
        for i in range(8):
            scr[b, i] = C[i]
        for i in range(8):
            for t in range(i, 8):
                s[t, i] = jnp.broadcast_to(scr[b, i, pl.ds(t, 1), :], (8, 128))
        scr[b, 8] = S[b]
        scr[b, 9] = E[b]
        R = [jnp.broadcast_to(scr[b, 8, pl.ds(i, 1), :], (8, 128)) for i in range(8)]
        Q = [jnp.broadcast_to(scr[b, 9, pl.ds(i, 1), :], (8, 128)) for i in range(8)]
        rd, l = [], {}
        for i in range(8):
            rd.append(1.0 / s[i, i])
            for t in range(i+1, 8):
                l[t, i] = s[t, i] * rd[i]
            for u in range(i+1, 8):
                for t in range(u, 8):
                    s[t, u] = s[t, u] - l[t, i] * s[u, i]
            for t in range(i+1, 8):
                R[t] = R[t] - l[t, i] * R[i]
                Q[t] = Q[t] - l[t, i] * Q[i]
        ru = [lax.rsqrt(s[i, i]) for i in range(8)]
        Uo = R[0] * ru[0]; Vo = Q[0] * ru[0]
        for i in range(1, 8):
            Uo = jnp.where(sub == i, R[i] * ru[i], Uo)
            Vo = jnp.where(sub == i, Q[i] * ru[i], Vo)
        U.append(Uo); V.append(Vo)
        if b == n-1: break
        Z = [None]*8; Y = [None]*8
        for i in range(7, -1, -1):
            z = R[i] * rd[i]; y = Q[i] * rd[i]
            for t in range(7, i, -1):
                z = z - l[t, i] * Z[t]
                y = y - l[t, i] * Y[t]
            Z[i] = z; Y[i] = y
        for g in range(b+1, n):
            c = [bl(S[g], 8*b+i) for i in range(8)]
            a0 = c[0]*Z[0]; a1 = c[1]*Z[1]; e0 = c[0]*Y[0]; e1 = c[1]*Y[1]
            for i in range(2, 8, 2):
                a0 = a0 + c[i]*Z[i]; a1 = a1 + c[i+1]*Z[i+1]
                e0 = e0 + c[i]*Y[i]; e1 = e1 + c[i+1]*Y[i+1]
            S[g] = S[g] - (a0 + a1)
            E[g] = E[g] - (e0 + e1)
    return U, V


def dt(a, b):
    return lax.dot_general(a, b, (((1,), (1,)), ((), ())), precision=HI, preferred_element_type=jnp.float32)


def whole_kernel(x_ref, reg_ref, out_ref, tile_ref, m_ref, band_ref, L, B, T, Vs, scr, xg, wc, wt, prod, parts, halves,
                 ring_send, ring_recv, pair_send, pair_recv, part_send, part_recv, hub_send, hub_recv,
                 near_send, near_recv, top_send, top_recv, row_send, row_recv, core_send, core_recv):
    r = lax.axis_index("row")
    c = lax.axis_index("col")
    h = c // RING
    z = c % RING
    q = z % 8
    other = 1 - h
    chip = r // 2
    core = r % 2
    sibling = 2 * chip + 1 - core
    partner = other * RING + z

    def along(distance):
        return h * RING + (z + distance + RING) % RING

    right, left = along(1), along(-1)
    hubs = (partner, along(8), other * RING + (z + 8) % RING)
    near = (1, 2, 3, 4, -3, -2, -1)

    barrier = pltpu.get_barrier_semaphore()
    for place in hubs + tuple(along(d) for d in near) + (along(-4),):
        pl.semaphore_signal(barrier, inc=1, device_id=(r, place), device_id_type=MESH)
    for step in range(1, 16):
        pl.semaphore_signal(barrier, inc=1, device_id=((r + step) % 16, c), device_id_type=MESH)
    pl.semaphore_wait(barrier, 26)

    def remote(src, dst, send, recv, device):
        return pltpu.make_async_remote_copy(
            src_ref=src, dst_ref=dst, send_sem=send, recv_sem=recv, device_id=device, device_id_type=MESH
        )

    swap = remote(x_ref, wc.at[h], pair_send.at[0], pair_recv.at[0], (r, partner))

    def ring_copy(way, step, chunk):
        owner = (z - step + 1 + RING) % RING if way == 0 else (z + step - 1) % RING
        rows = pl.ds(128 // CHUNKS * chunk, 128 // CHUNKS)
        src = x_ref.at[rows] if step == 1 else xg.at[owner, rows]
        return remote(src, xg.at[owner, rows], ring_send.at[way, step - 1, chunk],
                      ring_recv.at[way, step - 1, chunk], (r, right if way == 0 else left))

    steps = (8, 7)
    for chunk in range(CHUNKS):
        for way in range(2):
            ring_copy(way, 1, chunk).start()
    swap.start()
    wc[h] = x_ref[...]

    def multiply(owner, block):
        product = jnp.dot(block, wt[...], preferred_element_type=jnp.float32)
        prod[owner] = product.reshape(2, 64, 256)
        place = owner % 8
        half_k = owner // 8
        for to in range(2):
            mine = jnp.logical_and(place == chip, core == to)

            @pl.when(jnp.logical_not(mine))
            def _():
                remote(prod.at[owner, to], parts.at[half_k, r], part_send, part_recv.at[half_k],
                       (2 * place + to, c)).start()

            @pl.when(mine)
            def _():
                parts[half_k, r] = prod[owner, to]

    for step in range(1, 9):
        for chunk in range(CHUNKS):
            for way in range(2):
                if step <= steps[way]:
                    ring_copy(way, step, chunk).wait_recv()
                    if step < steps[way]:
                        ring_copy(way, step + 1, chunk).start()
        if step == 1:
            swap.wait()
            wt[...] = wc[...].reshape(256, 512).T
            multiply(z, x_ref[...])
        for way in range(2):
            if step <= steps[way]:
                owner = (z - step + RING) % RING if way == 0 else (z + step) % RING
                multiply(owner, xg[owner])

    lane = lax.broadcasted_iota(jnp.int32, (64, 128), 1)
    sub = lax.broadcasted_iota(jnp.int32, (64, 128), 0)
    for half_k in range(2):
        pltpu.make_async_copy(parts.at[half_k, pl.ds(0, 15)], parts.at[half_k, pl.ds(0, 15)], part_recv.at[half_k]).wait()
        total = parts[half_k, 0]
        for source in range(1, 16):
            total = total + parts[half_k, source]
        for side in range(2):
            block = total[:, 128 * side:128 * side + 128]
            hit = jnp.logical_and(chip + 8 * half_k == z, h == side)
            diagonal = jnp.logical_and(lane == sub + 64 * core, hit)
            halves[side, half_k] = block + jnp.where(diagonal, jnp.broadcast_to(reg_ref[...], (64, 128)), 0.0)

    give = remote(halves.at[other], tile_ref.at[pl.ds(2 * h, 2)], pair_send.at[1], pair_recv.at[1], (r, partner))
    lead = [remote(halves.at[0, 0], m_ref.at[chip, core, q], hub_send.at[0, i], hub_recv.at[0], (r, hubs[i])) for i in range(3)]
    second = [remote(halves.at[0, 1], band_ref.at[q, 0], hub_send.at[1, i], hub_recv.at[1], (r, hubs[i])) for i in range(3)]
    third = [remote(halves.at[0], band_ref.at[q, pl.ds(1, 2)], hub_send.at[2, i], hub_recv.at[2], (r, hubs[i])) for i in range(3)]
    source0 = jnp.logical_and(z < 8, h == 0)
    source1 = jnp.logical_and(z < 8, h == 1)

    @pl.when(source0)
    def _():
        for copy in lead:
            copy.start()
        m_ref[chip, core, q] = halves[0, 0]

    give.start()

    @pl.when(source0)
    def _():
        for copy in second:
            copy.start()
        band_ref[q, 0] = halves[0, 1]

    @pl.when(source1)
    def _():
        for copy in third:
            copy.start()
        band_ref[q, pl.ds(1, 2)] = halves[0]

    tile_ref[pl.ds(2 * h, 2)] = halves[h]

    def row_copy(group, step):
        at, count, _ = GROUPS[group]
        part = m_ref.at[chip, core, pl.ds(at, count)]
        return remote(part, part, row_send.at[group, step - 1], row_recv.at[group], ((r + 2 * step) % 16, c))

    def row_sends(group, act):
        def each():
            for step in range(1, 8):
                act(row_copy(group, step))

        if GROUPS[group][2] == 0:
            each()
        else:
            pl.when(chip >= GROUPS[group][2])(each)

    def core_copy(group):
        at, count, low = GROUPS[group]
        part = m_ref.at[pl.ds(low, 8 - low), core, pl.ds(at, count)]
        return remote(part, part, core_send.at[group], core_recv.at[group], (sibling, c))

    def row_pass(group):
        at, count, low = GROUPS[group]

        def arrive(sources):
            part = m_ref.at[pl.ds(0, sources), 0, pl.ds(at, count)]
            pltpu.make_async_copy(part, part, row_recv.at[group]).wait()

        if low == 0:
            arrive(7)
        else:
            pl.when(chip >= low)(lambda: arrive(7 - low))
            pl.when(chip < low)(lambda: arrive(8 - low))
        core_copy(group).start()

    def top_copy(band, step):
        part = m_ref.at[0, band, 0]
        return remote(part, part, top_send.at[step - 1], top_recv.at[band], ((r + step) % 16, c))

    def top_sends(act):
        for band in range(2):
            @pl.when(r == band)
            def _():
                for step in range(1, 16):
                    act(top_copy(band, step))

    @pl.when(jnp.logical_not(source0))
    def _():
        lead[0].wait_recv()

    mine = m_ref.at[chip, core, q]
    near_copies = [remote(mine, mine, near_send.at[0, i], near_recv.at[0, i], (r, along(d))) for i, d in enumerate(near)]
    band_copies = [remote(band_ref.at[q], band_ref.at[q], near_send.at[1, i], near_recv.at[1, i], (r, along(d)))
                   for i, d in enumerate(near)]

    @pl.when(q < 2)
    def _():
        for copy in near_copies:
            copy.start()

    give.wait()
    m_ref[chip, core, 8] = tile_ref[0]
    row_sends(OWN, lambda copy: copy.start())
    for i in range(7):
        pl.when(q == i + 1)(near_copies[i].wait_recv)
    top_sends(lambda copy: copy.start())
    row_sends(0, lambda copy: copy.start())
    for i in range(7):
        pl.when(q == (i + 2) % 8)(near_copies[i].wait_recv)
    row_sends(1, lambda copy: copy.start())

    @pl.when(q >= 2)
    def _():
        for copy in near_copies:
            copy.start()

    @pl.when(jnp.logical_not(source0))
    def _():
        second[0].wait_recv()

    @pl.when(jnp.logical_not(source1))
    def _():
        third[0].wait_recv()

    for copy in band_copies:
        copy.start()

    for band in range(2):
        @pl.when(r != band)
        def _():
            top_copy(band, 1).wait_recv()

    lane = lax.broadcasted_iota(jnp.int32, (8, 128), 1)
    sub = lax.broadcasted_iota(jnp.int32, (8, 128), 0)
    E0 = [jnp.where(lane == sub + 8 * g, 1.0, 0.0).astype(jnp.float32) for g in range(16)]

    def further(K):
        k0 = 128 * K
        value = jnp.concatenate([band_ref[K].reshape(192, 128), m_ref[K, :, 8].reshape(128, 128).T], 0)
        if K > 0:
            value = value - dt(L[pl.ds(1024, 320), pl.ds(0, k0)], L[pl.ds(k0, 128), pl.ds(0, k0)])
        L[pl.ds(1024, 320), pl.ds(k0, 128)] = dt(value, Vs[K])

    def middle(J):
        if J == 0:
            row_pass(0)
            row_pass(OWN)
        elif J == 1:
            row_pass(2)
        elif J == 2:
            row_pass(3)

    def after(J):
        if J == 0:
            row_pass(1)
            for i in range(7):
                pl.when(jnp.logical_and(q != i + 1, q != (i + 2) % 8))(near_copies[i].wait_recv)
            row_sends(2, lambda copy: copy.start())
            row_sends(3, lambda copy: copy.start())
            core_copy(0).wait_recv()
            B[pl.ds(128, 896), :] = m_ref[1:, :, 0].reshape(896, 128)
            core_copy(1).wait_recv()
        elif J == 1:
            core_copy(2).wait_recv()
        elif J == 3:
            core_copy(3).wait_recv()
            core_copy(OWN).wait_recv()
            for copy in band_copies:
                copy.wait_recv()

    B[pl.ds(0, 128), :] = m_ref[0, :, 0].reshape(128, 128)
    for J in range(8):
        j0 = 128 * J
        r0 = j0 + 128
        r1 = r0 + 128
        S = [B[pl.ds(j0 + 8 * g, 8), :] for g in range(16)]
        U, V = factor(S, E0, scr, lambda: middle(J))
        after(J)
        if J < 7:
            value = m_ref[J + 1:, :, J + 1].reshape(1024 - r0, 128)
            if J > 0:
                value = value - dt(L[pl.ds(r0, 1024 - r0), pl.ds(0, j0)], L[pl.ds(r0, 128), pl.ds(0, j0)])
            T[pl.ds(r0, 1024 - r0), :] = value
        for K in FURTHER[J]:
            further(K)
        Um = jnp.concatenate([jnp.where(lane >= sub + 8 * g, U[g], 0.0) for g in range(16)], 0)
        Vm = jnp.concatenate(V, 0)
        Vs[J] = Vm
        L[pl.ds(j0, 128), pl.ds(j0, 128)] = Um.T
        if J < 7:
            Pn = dt(B[pl.ds(r0, 128), :], Vm)
            L[pl.ds(r0, 128), pl.ds(j0, 128)] = Pn
            B[pl.ds(r0, 128), :] = T[pl.ds(r0, 128), :] - dt(Pn, Pn)
        if J < 6:
            Pr = dt(B[pl.ds(r1, 1024 - r1), :], Vm)
            L[pl.ds(r1, 1024 - r1), pl.ds(j0, 128)] = Pr
            B[pl.ds(r1, 1024 - r1), :] = T[pl.ds(r1, 1024 - r1), :] - dt(Pr, Pn)
    further(7)
    for J in range(7):
        L[pl.ds(128 * J, 128), pl.ds(128 * (J + 1), 128 * (7 - J))] = jnp.zeros((128, 128 * (7 - J)), jnp.float32)
    tr = tile_ref[1:].reshape(192, 128) - dt(L[pl.ds(1024, 192), :], L[pl.ds(1216, 128), :])
    column = pl.multiple_of(jnp.minimum(c, 7) * 128, 128)
    top = L[pl.ds(pl.multiple_of(r * 64, 64), 64), pl.ds(column, 128)]
    solved = L[pl.ds(1024, 192), pl.ds(column, 128)]
    in_panel = c < 8
    out_ref[0] = jnp.where(in_panel, top, 0.0)
    out_ref[1:] = jnp.where(in_panel, solved, tr).reshape(3, 64, 128)

    top_sends(lambda copy: copy.wait_send())
    for group in range(len(GROUPS)):
        row_sends(group, lambda copy: copy.wait_send())
        core_copy(group).wait_send()
    for way in range(2):
        for step in range(1, steps[way] + 1):
            for chunk in range(CHUNKS):
                ring_copy(way, step, chunk).wait_send()
    for copy in near_copies + band_copies:
        copy.wait_send()

    @pl.when(source0)
    def _():
        for copy in lead + second:
            copy.wait_send()

    @pl.when(source1)
    def _():
        for copy in third:
            copy.wait_send()

    pltpu.make_async_copy(prod.at[pl.ds(0, 15)], prod.at[pl.ds(0, 15)], part_send).wait()


def body(interactions, regular):
    vmem = pl.BlockSpec(memory_space=pltpu.VMEM)
    dma = pltpu.SemaphoreType.DMA
    rows = 1024 + 192 + 128
    return pl.pallas_call(
        whole_kernel,
        out_shape=jax.ShapeDtypeStruct((4, 64, 128), jnp.float32),
        in_specs=[vmem, vmem],
        out_specs=vmem,
        scratch_shapes=[
            pltpu.VMEM((4, 64, 128), jnp.float32),
            pltpu.VMEM((8, 2, 9, 64, 128), jnp.float32),
            pltpu.VMEM((8, 3, 64, 128), jnp.float32),
            pltpu.VMEM((rows, PANEL), jnp.float32),
            pltpu.VMEM((rows, 128), jnp.float32),
            pltpu.VMEM((rows, 128), jnp.float32),
            pltpu.VMEM((8, 128, 128), jnp.float32),
            pltpu.VMEM((16, 10, 8, 128), jnp.float32),
            pltpu.VMEM((RING, 128, 512), jnp.bfloat16),
            pltpu.VMEM((2, 128, 512), jnp.bfloat16),
            pltpu.VMEM((512, 256), jnp.bfloat16),
            pltpu.VMEM((RING, 2, 64, 256), jnp.float32),
            pltpu.VMEM((2, 16, 64, 256), jnp.float32),
            pltpu.VMEM((2, 2, 64, 128), jnp.float32),
            dma((2, 8, CHUNKS)),
            dma((2, 8, CHUNKS)),
            dma((2,)),
            dma((2,)),
            dma,
            dma((2,)),
            dma((3, 3)),
            dma((3,)),
            dma((2, 7)),
            dma((2, 7)),
            dma((15,)),
            dma((2,)),
            dma((len(GROUPS), 7)),
            dma((len(GROUPS),)),
            dma((len(GROUPS),)),
            dma((len(GROUPS),)),
        ],
        compiler_params=pltpu.CompilerParams(
            collective_id=0, has_side_effects=True, vmem_limit_bytes=50 * 1024 * 1024
        ),
        name="whole",
    )(interactions, regular.reshape(1, 128))


def solution(mesh):
    return jax.shard_map(
        body,
        mesh=mesh,
        in_specs=(P("col", "row"), P("col")),
        out_specs=P(None, "row", "col"),
        check_vma=False,
    )
```

```python
import jax
import jax.numpy as jnp
from jax import lax
from jax.experimental import pallas as pl
from jax.experimental.pallas import tpu as pltpu
from jax.sharding import PartitionSpec as P

PANEL = 1024
RING = 16
CHUNKS = 2
GROUPS = ((0, 1, 1), (1, 1, 1), (2, 2, 2), (4, 4, 4), (8, 1, 0))
OWN = 4
FURTHER = ((), (), (), (), (0, 1), (2, 3), (4, 5), (6,))
HI = lax.Precision.HIGHEST
MESH = pl.DeviceIdType.MESH


def bl(x, lane):
    return jnp.broadcast_to(x[:, lane:lane+1], (8, 128))
def bs(x, row):
    return jnp.broadcast_to(x[row:row+1, :], (8, 128))

def factor(S, E, scr, middle):
    sub = lax.broadcasted_iota(jnp.int32, (8, 128), 0)
    U, V = [], []
    n = len(S)
    S = list(S); E = list(E)
    for b in range(n):
        if b == n // 2:
            middle()
        C = [bl(S[b], 8*b+i) for i in range(8)]
        s = {}
        for i in range(8):
            scr[b, i] = C[i]
        for i in range(8):
            for t in range(i, 8):
                s[t, i] = jnp.broadcast_to(scr[b, i, pl.ds(t, 1), :], (8, 128))
        scr[b, 8] = S[b]
        scr[b, 9] = E[b]
        R = [jnp.broadcast_to(scr[b, 8, pl.ds(i, 1), :], (8, 128)) for i in range(8)]
        Q = [jnp.broadcast_to(scr[b, 9, pl.ds(i, 1), :], (8, 128)) for i in range(8)]
        rd, l = [], {}
        for i in range(8):
            rd.append(1.0 / s[i, i])
            for t in range(i+1, 8):
                l[t, i] = s[t, i] * rd[i]
            for u in range(i+1, 8):
                for t in range(u, 8):
                    s[t, u] = s[t, u] - l[t, i] * s[u, i]
            for t in range(i+1, 8):
                R[t] = R[t] - l[t, i] * R[i]
                Q[t] = Q[t] - l[t, i] * Q[i]
        ru = [lax.rsqrt(s[i, i]) for i in range(8)]
        Uo = R[0] * ru[0]; Vo = Q[0] * ru[0]
        for i in range(1, 8):
            Uo = jnp.where(sub == i, R[i] * ru[i], Uo)
            Vo = jnp.where(sub == i, Q[i] * ru[i], Vo)
        U.append(Uo); V.append(Vo)
        if b == n-1: break
        Z = [None]*8; Y = [None]*8
        for i in range(7, -1, -1):
            z = R[i] * rd[i]; y = Q[i] * rd[i]
            for t in range(7, i, -1):
                z = z - l[t, i] * Z[t]
                y = y - l[t, i] * Y[t]
            Z[i] = z; Y[i] = y
        for g in range(b+1, n):
            c = [bl(S[g], 8*b+i) for i in range(8)]
            a0 = c[0]*Z[0]; a1 = c[1]*Z[1]; e0 = c[0]*Y[0]; e1 = c[1]*Y[1]
            for i in range(2, 8, 2):
                a0 = a0 + c[i]*Z[i]; a1 = a1 + c[i+1]*Z[i+1]
                e0 = e0 + c[i]*Y[i]; e1 = e1 + c[i+1]*Y[i+1]
            S[g] = S[g] - (a0 + a1)
            E[g] = E[g] - (e0 + e1)
    return U, V


def dt(a, b):
    return lax.dot_general(a, b, (((1,), (1,)), ((), ())), precision=HI, preferred_element_type=jnp.float32)


def whole_kernel(x_ref, reg_ref, out_ref, tile_ref, m_ref, band_ref, L, B, T, Vs, scr, xg, wc, wt, prod, parts, halves,
                 ring_send, ring_recv, pair_send, pair_recv, part_send, part_recv, hub_send, hub_recv,
                 near_send, near_recv, top_send, top_recv, row_send, row_recv, core_send, core_recv):
    r = lax.axis_index("row")
    c = lax.axis_index("col")
    h = c // RING
    z = c % RING
    q = z % 8
    other = 1 - h
    chip = r // 2
    core = r % 2
    sibling = 2 * chip + 1 - core
    partner = other * RING + z

    def along(distance):
        return h * RING + (z + distance + RING) % RING

    right, left = along(1), along(-1)
    hubs = (partner, along(8), other * RING + (z + 8) % RING)
    near = (1, 2, 3, 4, -3, -2, -1)

    barrier = pltpu.get_barrier_semaphore()
    for place in hubs + tuple(along(d) for d in near) + (along(-4),):
        pl.semaphore_signal(barrier, inc=1, device_id=(r, place), device_id_type=MESH)
    for step in range(1, 16):
        pl.semaphore_signal(barrier, inc=1, device_id=((r + step) % 16, c), device_id_type=MESH)
    pl.semaphore_wait(barrier, 26)

    def remote(src, dst, send, recv, device):
        return pltpu.make_async_remote_copy(
            src_ref=src, dst_ref=dst, send_sem=send, recv_sem=recv, device_id=device, device_id_type=MESH
        )

    swap = remote(x_ref, wc.at[h], pair_send.at[0], pair_recv.at[0], (r, partner))

    def ring_copy(way, step, chunk):
        owner = (z - step + 1 + RING) % RING if way == 0 else (z + step - 1) % RING
        rows = pl.ds(128 // CHUNKS * chunk, 128 // CHUNKS)
        src = x_ref.at[rows] if step == 1 else xg.at[owner, rows]
        return remote(src, xg.at[owner, rows], ring_send.at[way, step - 1, chunk],
                      ring_recv.at[way, step - 1, chunk], (r, right if way == 0 else left))

    steps = (8, 7)
    for chunk in range(CHUNKS):
        for way in range(2):
            ring_copy(way, 1, chunk).start()
    swap.start()
    wc[h] = x_ref[...]

    def multiply(owner, block):
        product = jnp.dot(block, wt[...], preferred_element_type=jnp.float32)
        prod[owner] = product.reshape(2, 64, 256)
        place = owner % 8
        half_k = owner // 8
        for to in range(2):
            mine = jnp.logical_and(place == chip, core == to)

            @pl.when(jnp.logical_not(mine))
            def _():
                remote(prod.at[owner, to], parts.at[half_k, r], part_send, part_recv.at[half_k],
                       (2 * place + to, c)).start()

            @pl.when(mine)
            def _():
                parts[half_k, r] = prod[owner, to]

    for step in range(1, 9):
        for chunk in range(CHUNKS):
            for way in range(2):
                if step <= steps[way]:
                    ring_copy(way, step, chunk).wait_recv()
                    if step < steps[way]:
                        ring_copy(way, step + 1, chunk).start()
        if step == 1:
            swap.wait()
            wt[...] = wc[...].reshape(256, 512).T
            multiply(z, x_ref[...])
        for way in range(2):
            if step <= steps[way]:
                owner = (z - step + RING) % RING if way == 0 else (z + step) % RING
                multiply(owner, xg[owner])

    lane = lax.broadcasted_iota(jnp.int32, (64, 128), 1)
    sub = lax.broadcasted_iota(jnp.int32, (64, 128), 0)
    for half_k in range(2):
        pltpu.make_async_copy(parts.at[half_k, pl.ds(0, 15)], parts.at[half_k, pl.ds(0, 15)], part_recv.at[half_k]).wait()
        total = parts[half_k, 0]
        for source in range(1, 16):
            total = total + parts[half_k, source]
        for side in range(2):
            block = total[:, 128 * side:128 * side + 128]
            hit = jnp.logical_and(chip + 8 * half_k == z, h == side)
            diagonal = jnp.logical_and(lane == sub + 64 * core, hit)
            halves[side, half_k] = block + jnp.where(diagonal, jnp.broadcast_to(reg_ref[...], (64, 128)), 0.0)

    give = remote(halves.at[other], tile_ref.at[pl.ds(2 * h, 2)], pair_send.at[1], pair_recv.at[1], (r, partner))
    lead = [remote(halves.at[0, 0], m_ref.at[chip, core, q], hub_send.at[0, i], hub_recv.at[0], (r, hubs[i])) for i in range(3)]
    second = [remote(halves.at[0, 1], band_ref.at[q, 0], hub_send.at[1, i], hub_recv.at[1], (r, hubs[i])) for i in range(3)]
    third = [remote(halves.at[0], band_ref.at[q, pl.ds(1, 2)], hub_send.at[2, i], hub_recv.at[2], (r, hubs[i])) for i in range(3)]
    source0 = jnp.logical_and(z < 8, h == 0)
    source1 = jnp.logical_and(z < 8, h == 1)

    @pl.when(source0)
    def _():
        for copy in lead:
            copy.start()
        m_ref[chip, core, q] = halves[0, 0]

    give.start()

    @pl.when(source0)
    def _():
        for copy in second:
            copy.start()
        band_ref[q, 0] = halves[0, 1]

    @pl.when(source1)
    def _():
        for copy in third:
            copy.start()
        band_ref[q, pl.ds(1, 2)] = halves[0]

    tile_ref[pl.ds(2 * h, 2)] = halves[h]

    def row_copy(group, step):
        at, count, _ = GROUPS[group]
        part = m_ref.at[chip, core, pl.ds(at, count)]
        return remote(part, part, row_send.at[group, step - 1], row_recv.at[group], ((r + 2 * step) % 16, c))

    def row_sends(group, act):
        def each():
            for step in range(1, 8):
                act(row_copy(group, step))

        if GROUPS[group][2] == 0:
            each()
        else:
            pl.when(chip >= GROUPS[group][2])(each)

    def core_copy(group):
        at, count, low = GROUPS[group]
        part = m_ref.at[pl.ds(low, 8 - low), core, pl.ds(at, count)]
        return remote(part, part, core_send.at[group], core_recv.at[group], (sibling, c))

    def row_pass(group):
        at, count, low = GROUPS[group]

        def arrive(sources):
            part = m_ref.at[pl.ds(0, sources), 0, pl.ds(at, count)]
            pltpu.make_async_copy(part, part, row_recv.at[group]).wait()

        if low == 0:
            arrive(7)
        else:
            pl.when(chip >= low)(lambda: arrive(7 - low))
            pl.when(chip < low)(lambda: arrive(8 - low))
        core_copy(group).start()

    def top_copy(band, step):
        part = m_ref.at[0, band, 0]
        return remote(part, part, top_send.at[step - 1], top_recv.at[band], ((r + step) % 16, c))

    def top_sends(act):
        for band in range(2):
            @pl.when(r == band)
            def _():
                for step in range(1, 16):
                    act(top_copy(band, step))

    @pl.when(jnp.logical_not(source0))
    def _():
        lead[0].wait_recv()

    mine = m_ref.at[chip, core, q]
    near_copies = [remote(mine, mine, near_send.at[0, i], near_recv.at[0, i], (r, along(d))) for i, d in enumerate(near)]
    band_copies = [remote(band_ref.at[q], band_ref.at[q], near_send.at[1, i], near_recv.at[1, i], (r, along(d)))
                   for i, d in enumerate(near)]

    @pl.when(q < 4)
    def _():
        for copy in near_copies:
            copy.start()

    give.wait()
    m_ref[chip, core, 8] = tile_ref[0]
    row_sends(OWN, lambda copy: copy.start())

    def near_wait(block):
        for i in range(7):
            pl.when(q == (i + 1 + block) % 8)(near_copies[i].wait_recv)

    near_wait(0)
    top_sends(lambda copy: copy.start())
    row_sends(0, lambda copy: copy.start())
    near_wait(1)
    row_sends(1, lambda copy: copy.start())
    near_wait(2)
    near_wait(3)
    row_sends(2, lambda copy: copy.start())

    @pl.when(q >= 4)
    def _():
        for copy in near_copies:
            copy.start()

    @pl.when(jnp.logical_not(source0))
    def _():
        second[0].wait_recv()

    @pl.when(jnp.logical_not(source1))
    def _():
        third[0].wait_recv()

    for band in range(2):
        @pl.when(r != band)
        def _():
            top_copy(band, 1).wait_recv()

    lane = lax.broadcasted_iota(jnp.int32, (8, 128), 1)
    sub = lax.broadcasted_iota(jnp.int32, (8, 128), 0)
    E0 = [jnp.where(lane == sub + 8 * g, 1.0, 0.0).astype(jnp.float32) for g in range(16)]

    def further(K):
        k0 = 128 * K
        value = jnp.concatenate([band_ref[K].reshape(192, 128), m_ref[K, :, 8].reshape(128, 128).T], 0)
        if K > 0:
            value = value - dt(L[pl.ds(1024, 320), pl.ds(0, k0)], L[pl.ds(k0, 128), pl.ds(0, k0)])
        L[pl.ds(1024, 320), pl.ds(k0, 128)] = dt(value, Vs[K])

    def middle(J):
        if J == 0:
            row_pass(0)
        elif J == 1:
            row_pass(2)
            for block in range(4, 8):
                near_wait(block)
            row_sends(3, lambda copy: copy.start())
        elif J == 2:
            row_pass(OWN)
        elif J == 3:
            row_pass(3)

    def after(J):
        if J == 0:
            for copy in band_copies:
                copy.start()
            row_pass(1)
            core_copy(0).wait_recv()
            B[pl.ds(128, 896), :] = m_ref[1:, :, 0].reshape(896, 128)
            core_copy(1).wait_recv()
        elif J == 1:
            core_copy(2).wait_recv()
        elif J == 3:
            core_copy(3).wait_recv()
            core_copy(OWN).wait_recv()
        elif J == 4:
            for copy in band_copies:
                copy.wait_recv()

    B[pl.ds(0, 128), :] = m_ref[0, :, 0].reshape(128, 128)
    for J in range(8):
        j0 = 128 * J
        r0 = j0 + 128
        r1 = r0 + 128
        S = [B[pl.ds(j0 + 8 * g, 8), :] for g in range(16)]
        U, V = factor(S, E0, scr, lambda: middle(J))
        after(J)
        if J < 7:
            value = m_ref[J + 1:, :, J + 1].reshape(1024 - r0, 128)
            if J > 0:
                value = value - dt(L[pl.ds(r0, 1024 - r0), pl.ds(0, j0)], L[pl.ds(r0, 128), pl.ds(0, j0)])
            T[pl.ds(r0, 1024 - r0), :] = value
        for K in FURTHER[J]:
            further(K)
        if J == 7:
            T[pl.ds(0, 192), :] = tile_ref[1:].reshape(192, 128) - dt(
                L[pl.ds(1024, 192), pl.ds(0, 896)], L[pl.ds(1216, 128), pl.ds(0, 896)])
        Um = jnp.concatenate([jnp.where(lane >= sub + 8 * g, U[g], 0.0) for g in range(16)], 0)
        Vm = jnp.concatenate(V, 0)
        Vs[J] = Vm
        L[pl.ds(j0, 128), pl.ds(j0, 128)] = Um.T
        if J < 7:
            Pn = dt(B[pl.ds(r0, 128), :], Vm)
            L[pl.ds(r0, 128), pl.ds(j0, 128)] = Pn
            B[pl.ds(r0, 128), :] = T[pl.ds(r0, 128), :] - dt(Pn, Pn)
        if J < 6:
            Pr = dt(B[pl.ds(r1, 1024 - r1), :], Vm)
            L[pl.ds(r1, 1024 - r1), pl.ds(j0, 128)] = Pr
            B[pl.ds(r1, 1024 - r1), :] = T[pl.ds(r1, 1024 - r1), :] - dt(Pr, Pn)
    further(7)
    tr = T[pl.ds(0, 192), :] - dt(L[pl.ds(1024, 192), pl.ds(896, 128)], L[pl.ds(1216, 128), pl.ds(896, 128)])
    column = pl.multiple_of(jnp.minimum(c, 7) * 128, 128)
    top = L[pl.ds(pl.multiple_of(r * 64, 64), 64), pl.ds(column, 128)]
    solved = L[pl.ds(1024, 192), pl.ds(column, 128)]
    in_panel = c < 8
    below = lax.broadcasted_iota(jnp.int32, (64, 128), 1) + column <= lax.broadcasted_iota(jnp.int32, (64, 128), 0) + r * 64
    out_ref[0] = jnp.where(jnp.logical_and(in_panel, below), top, 0.0)
    out_ref[1:] = jnp.where(in_panel, solved, tr).reshape(3, 64, 128)

    top_sends(lambda copy: copy.wait_send())
    for group in range(len(GROUPS)):
        row_sends(group, lambda copy: copy.wait_send())
        core_copy(group).wait_send()
    for way in range(2):
        for step in range(1, steps[way] + 1):
            for chunk in range(CHUNKS):
                ring_copy(way, step, chunk).wait_send()
    for copy in near_copies + band_copies:
        copy.wait_send()

    @pl.when(source0)
    def _():
        for copy in lead + second:
            copy.wait_send()

    @pl.when(source1)
    def _():
        for copy in third:
            copy.wait_send()

    pltpu.make_async_copy(prod.at[pl.ds(0, 15)], prod.at[pl.ds(0, 15)], part_send).wait()


def body(interactions, regular):
    vmem = pl.BlockSpec(memory_space=pltpu.VMEM)
    dma = pltpu.SemaphoreType.DMA
    rows = 1024 + 192 + 128
    return pl.pallas_call(
        whole_kernel,
        out_shape=jax.ShapeDtypeStruct((4, 64, 128), jnp.float32),
        in_specs=[vmem, vmem],
        out_specs=vmem,
        scratch_shapes=[
            pltpu.VMEM((4, 64, 128), jnp.float32),
            pltpu.VMEM((8, 2, 9, 64, 128), jnp.float32),
            pltpu.VMEM((8, 3, 64, 128), jnp.float32),
            pltpu.VMEM((rows, PANEL), jnp.float32),
            pltpu.VMEM((rows, 128), jnp.float32),
            pltpu.VMEM((rows, 128), jnp.float32),
            pltpu.VMEM((8, 128, 128), jnp.float32),
            pltpu.VMEM((16, 10, 8, 128), jnp.float32),
            pltpu.VMEM((RING, 128, 512), jnp.bfloat16),
            pltpu.VMEM((2, 128, 512), jnp.bfloat16),
            pltpu.VMEM((512, 256), jnp.bfloat16),
            pltpu.VMEM((RING, 2, 64, 256), jnp.float32),
            pltpu.VMEM((2, 16, 64, 256), jnp.float32),
            pltpu.VMEM((2, 2, 64, 128), jnp.float32),
            dma((2, 8, CHUNKS)),
            dma((2, 8, CHUNKS)),
            dma((2,)),
            dma((2,)),
            dma,
            dma((2,)),
            dma((3, 3)),
            dma((3,)),
            dma((2, 7)),
            dma((2, 7)),
            dma((15,)),
            dma((2,)),
            dma((len(GROUPS), 7)),
            dma((len(GROUPS),)),
            dma((len(GROUPS),)),
            dma((len(GROUPS),)),
        ],
        compiler_params=pltpu.CompilerParams(
            collective_id=0, has_side_effects=True, vmem_limit_bytes=50 * 1024 * 1024
        ),
        name="whole",
    )(interactions, regular.reshape(1, 128))


def solution(mesh):
    return jax.shard_map(
        body,
        mesh=mesh,
        in_specs=(P("col", "row"), P("col")),
        out_specs=P(None, "row", "col"),
        check_vma=False,
    )
```

```python
import jax
import jax.numpy as jnp
from jax import lax
from jax.experimental import pallas as pl
from jax.experimental.pallas import tpu as pltpu
from jax.sharding import PartitionSpec as P

PANEL = 1024
RING = 16
CHUNKS = 2
GROUPS = ((0, 1, 1), (1, 1, 1), (2, 2, 2), (4, 4, 4), (8, 1, 0))
OWN = 4
FURTHER = ((), (), (), (), (0, 1), (2, 3), (4, 5), (6,))
HI = lax.Precision.HIGHEST
MESH = pl.DeviceIdType.MESH


def bl(x, lane):
    return jnp.broadcast_to(x[:, lane:lane+1], (8, 128))
def bs(x, row):
    return jnp.broadcast_to(x[row:row+1, :], (8, 128))

def factor(S, E, scr, middle):
    sub = lax.broadcasted_iota(jnp.int32, (8, 128), 0)
    U, V = [], []
    n = len(S)
    S = list(S); E = list(E)
    for b in range(n):
        if b == n // 2:
            middle()
        C = [bl(S[b], 8*b+i) for i in range(8)]
        s = {}
        for i in range(8):
            scr[b, i] = C[i]
        for i in range(8):
            for t in range(i, 8):
                s[t, i] = jnp.broadcast_to(scr[b, i, pl.ds(t, 1), :], (8, 128))
        scr[b, 8] = S[b]
        scr[b, 9] = E[b]
        R = [jnp.broadcast_to(scr[b, 8, pl.ds(i, 1), :], (8, 128)) for i in range(8)]
        Q = [jnp.broadcast_to(scr[b, 9, pl.ds(i, 1), :], (8, 128)) for i in range(8)]
        rd, l = [], {}
        for i in range(8):
            rd.append(1.0 / s[i, i])
            for t in range(i+1, 8):
                l[t, i] = s[t, i] * rd[i]
            for u in range(i+1, 8):
                for t in range(u, 8):
                    s[t, u] = s[t, u] - l[t, i] * s[u, i]
            for t in range(i+1, 8):
                R[t] = R[t] - l[t, i] * R[i]
                Q[t] = Q[t] - l[t, i] * Q[i]
        ru = [lax.rsqrt(s[i, i]) for i in range(8)]
        Uo = R[0] * ru[0]; Vo = Q[0] * ru[0]
        for i in range(1, 8):
            Uo = jnp.where(sub == i, R[i] * ru[i], Uo)
            Vo = jnp.where(sub == i, Q[i] * ru[i], Vo)
        U.append(Uo); V.append(Vo)
        if b == n-1: break
        Z = [None]*8; Y = [None]*8
        for i in range(7, -1, -1):
            z = R[i] * rd[i]; y = Q[i] * rd[i]
            for t in range(7, i, -1):
                z = z - l[t, i] * Z[t]
                y = y - l[t, i] * Y[t]
            Z[i] = z; Y[i] = y
        for g in range(b+1, n):
            c = [bl(S[g], 8*b+i) for i in range(8)]
            a0 = c[0]*Z[0]; a1 = c[1]*Z[1]; e0 = c[0]*Y[0]; e1 = c[1]*Y[1]
            for i in range(2, 8, 2):
                a0 = a0 + c[i]*Z[i]; a1 = a1 + c[i+1]*Z[i+1]
                e0 = e0 + c[i]*Y[i]; e1 = e1 + c[i+1]*Y[i+1]
            S[g] = S[g] - (a0 + a1)
            E[g] = E[g] - (e0 + e1)
    return U, V


def dt(a, b):
    return lax.dot_general(a, b, (((1,), (1,)), ((), ())), precision=HI, preferred_element_type=jnp.float32)


def whole_kernel(x_ref, reg_ref, out_ref, tile_ref, m_ref, band_ref, L, B, T, Vs, scr, xg, wc, wt, prod, pair, parts, halves,
                 ring_send, ring_recv, pair_send, pair_recv, sib_send, sib_recv, part_send, part_recv, hub_send, hub_recv,
                 near_send, near_recv, top_send, top_recv, row_send, row_recv, core_send, core_recv):
    r = lax.axis_index("row")
    c = lax.axis_index("col")
    h = c // RING
    z = c % RING
    q = z % 8
    other = 1 - h
    chip = r // 2
    core = r % 2
    sibling = 2 * chip + 1 - core
    partner = other * RING + z

    def along(distance):
        return h * RING + (z + distance + RING) % RING

    right, left = along(1), along(-1)
    hubs = (partner, along(8), other * RING + (z + 8) % RING)
    near = (1, 2, 3, 4, -3, -2, -1)

    barrier = pltpu.get_barrier_semaphore()
    for place in hubs + tuple(along(d) for d in near) + (along(-4),):
        pl.semaphore_signal(barrier, inc=1, device_id=(r, place), device_id_type=MESH)
    for step in range(1, 16):
        pl.semaphore_signal(barrier, inc=1, device_id=((r + step) % 16, c), device_id_type=MESH)
    pl.semaphore_wait(barrier, 26)

    def remote(src, dst, send, recv, device):
        return pltpu.make_async_remote_copy(
            src_ref=src, dst_ref=dst, send_sem=send, recv_sem=recv, device_id=device, device_id_type=MESH
        )

    swap = remote(x_ref, wc.at[h], pair_send.at[0], pair_recv.at[0], (r, partner))

    def ring_copy(way, step, chunk):
        owner = (z - step + 1 + RING) % RING if way == 0 else (z + step - 1) % RING
        rows = pl.ds(128 // CHUNKS * chunk, 128 // CHUNKS)
        src = x_ref.at[rows] if step == 1 else xg.at[owner, rows]
        return remote(src, xg.at[owner, rows], ring_send.at[way, step - 1, chunk],
                      ring_recv.at[way, step - 1, chunk], (r, right if way == 0 else left))

    steps = (8, 7)
    for chunk in range(CHUNKS):
        for way in range(2):
            ring_copy(way, 1, chunk).start()
    swap.start()
    wc[h] = x_ref[...]

    def multiply(index, owner, block):
        product = jnp.dot(block, wt[...], preferred_element_type=jnp.float32)
        prod[owner] = product.reshape(2, 64, 256)
        remote(prod.at[owner, 1 - core], pair.at[owner], sib_send, sib_recv.at[index], (sibling, c)).start()

    def pass_on(index, owner):
        remote(prod.at[owner, 1 - core], pair.at[owner], sib_send, sib_recv.at[index], (sibling, c)).wait_recv()
        prod[owner, core] = prod[owner, core] + pair[owner]
        place = owner % 8
        half_k = owner // 8

        @pl.when(place != chip)
        def _():
            remote(prod.at[owner, core], parts.at[half_k, chip], part_send, part_recv.at[half_k],
                   (2 * place + core, c)).start()

        @pl.when(place == chip)
        def _():
            parts[half_k, chip] = prod[owner, core]

    def owners(step):
        if step == 0:
            return [(0, z)]
        both = [(2 * step - 1, (z - step + RING) % RING), (2 * step, (z + step) % RING)]
        return both if step < 8 else both[:1]

    for step in range(1, 9):
        for chunk in range(CHUNKS):
            for way in range(2):
                if step <= steps[way]:
                    ring_copy(way, step, chunk).wait_recv()
                    if step < steps[way]:
                        ring_copy(way, step + 1, chunk).start()
        if step == 1:
            swap.wait()
            wt[...] = wc[...].reshape(256, 512).T
            multiply(0, z, x_ref[...])
        for index, owner in owners(step):
            multiply(index, owner, xg[owner])
        for index, owner in owners(step - 1):
            pass_on(index, owner)
    for index, owner in owners(8):
        pass_on(index, owner)

    lane = lax.broadcasted_iota(jnp.int32, (64, 128), 1)
    sub = lax.broadcasted_iota(jnp.int32, (64, 128), 0)
    for half_k in range(2):
        pltpu.make_async_copy(parts.at[half_k, pl.ds(0, 7)], parts.at[half_k, pl.ds(0, 7)], part_recv.at[half_k]).wait()
        total = parts[half_k, 0]
        for source in range(1, 8):
            total = total + parts[half_k, source]
        for side in range(2):
            block = total[:, 128 * side:128 * side + 128]
            hit = jnp.logical_and(chip + 8 * half_k == z, h == side)
            diagonal = jnp.logical_and(lane == sub + 64 * core, hit)
            halves[side, half_k] = block + jnp.where(diagonal, jnp.broadcast_to(reg_ref[...], (64, 128)), 0.0)

    give = remote(halves.at[other], tile_ref.at[pl.ds(2 * h, 2)], pair_send.at[1], pair_recv.at[1], (r, partner))
    lead = [remote(halves.at[0, 0], m_ref.at[chip, core, q], hub_send.at[0, i], hub_recv.at[0], (r, hubs[i])) for i in range(3)]
    second = [remote(halves.at[0, 1], band_ref.at[q, 0], hub_send.at[1, i], hub_recv.at[1], (r, hubs[i])) for i in range(3)]
    third = [remote(halves.at[0], band_ref.at[q, pl.ds(1, 2)], hub_send.at[2, i], hub_recv.at[2], (r, hubs[i])) for i in range(3)]
    source0 = jnp.logical_and(z < 8, h == 0)
    source1 = jnp.logical_and(z < 8, h == 1)

    @pl.when(source0)
    def _():
        for copy in lead:
            copy.start()
        m_ref[chip, core, q] = halves[0, 0]

    give.start()

    @pl.when(source0)
    def _():
        for copy in second:
            copy.start()
        band_ref[q, 0] = halves[0, 1]

    @pl.when(source1)
    def _():
        for copy in third:
            copy.start()
        band_ref[q, pl.ds(1, 2)] = halves[0]

    tile_ref[pl.ds(2 * h, 2)] = halves[h]

    def row_copy(group, step):
        at, count, _ = GROUPS[group]
        part = m_ref.at[chip, core, pl.ds(at, count)]
        return remote(part, part, row_send.at[group, step - 1], row_recv.at[group], ((r + 2 * step) % 16, c))

    def row_sends(group, act):
        def each():
            for step in range(1, 8):
                act(row_copy(group, step))

        if GROUPS[group][2] == 0:
            each()
        else:
            pl.when(chip >= GROUPS[group][2])(each)

    def core_copy(group):
        at, count, low = GROUPS[group]
        part = m_ref.at[pl.ds(low, 8 - low), core, pl.ds(at, count)]
        return remote(part, part, core_send.at[group], core_recv.at[group], (sibling, c))

    def row_pass(group):
        at, count, low = GROUPS[group]

        def arrive(sources):
            part = m_ref.at[pl.ds(0, sources), 0, pl.ds(at, count)]
            pltpu.make_async_copy(part, part, row_recv.at[group]).wait()

        if low == 0:
            arrive(7)
        else:
            pl.when(chip >= low)(lambda: arrive(7 - low))
            pl.when(chip < low)(lambda: arrive(8 - low))
        core_copy(group).start()

    def top_copy(band, step):
        part = m_ref.at[0, band, 0]
        return remote(part, part, top_send.at[step - 1], top_recv.at[band], ((r + step) % 16, c))

    def top_sends(act):
        for band in range(2):
            @pl.when(r == band)
            def _():
                for step in range(1, 16):
                    act(top_copy(band, step))

    @pl.when(jnp.logical_not(source0))
    def _():
        lead[0].wait_recv()

    mine = m_ref.at[chip, core, q]
    near_copies = [remote(mine, mine, near_send.at[0, i], near_recv.at[0, i], (r, along(d))) for i, d in enumerate(near)]
    band_copies = [remote(band_ref.at[q], band_ref.at[q], near_send.at[1, i], near_recv.at[1, i], (r, along(d)))
                   for i, d in enumerate(near)]

    @pl.when(q < 4)
    def _():
        for copy in near_copies:
            copy.start()

    give.wait()
    m_ref[chip, core, 8] = tile_ref[0]
    row_sends(OWN, lambda copy: copy.start())

    def near_wait(block):
        for i in range(7):
            pl.when(q == (i + 1 + block) % 8)(near_copies[i].wait_recv)

    near_wait(0)
    top_sends(lambda copy: copy.start())
    row_sends(0, lambda copy: copy.start())
    near_wait(1)
    row_sends(1, lambda copy: copy.start())
    near_wait(2)
    near_wait(3)
    row_sends(2, lambda copy: copy.start())

    @pl.when(q >= 4)
    def _():
        for copy in near_copies:
            copy.start()

    @pl.when(jnp.logical_not(source0))
    def _():
        second[0].wait_recv()

    @pl.when(jnp.logical_not(source1))
    def _():
        third[0].wait_recv()

    for band in range(2):
        @pl.when(r != band)
        def _():
            top_copy(band, 1).wait_recv()

    lane = lax.broadcasted_iota(jnp.int32, (8, 128), 1)
    sub = lax.broadcasted_iota(jnp.int32, (8, 128), 0)
    E0 = [jnp.where(lane == sub + 8 * g, 1.0, 0.0).astype(jnp.float32) for g in range(16)]

    def further(K):
        k0 = 128 * K
        value = jnp.concatenate([band_ref[K].reshape(192, 128), m_ref[K, :, 8].reshape(128, 128).T], 0)
        if K > 0:
            value = value - dt(L[pl.ds(1024, 320), pl.ds(0, k0)], L[pl.ds(k0, 128), pl.ds(0, k0)])
        L[pl.ds(1024, 320), pl.ds(k0, 128)] = dt(value, Vs[K])

    def middle(J):
        if J == 0:
            row_pass(0)
        elif J == 1:
            row_pass(2)
            for block in range(4, 8):
                near_wait(block)
            row_sends(3, lambda copy: copy.start())
        elif J == 2:
            row_pass(OWN)
        elif J == 3:
            row_pass(3)

    def after(J):
        if J == 0:
            for copy in band_copies:
                copy.start()
            row_pass(1)
            core_copy(0).wait_recv()
            B[pl.ds(128, 896), :] = m_ref[1:, :, 0].reshape(896, 128)
            core_copy(1).wait_recv()
        elif J == 1:
            core_copy(2).wait_recv()
        elif J == 3:
            core_copy(3).wait_recv()
            core_copy(OWN).wait_recv()
        elif J == 4:
            for copy in band_copies:
                copy.wait_recv()

    B[pl.ds(0, 128), :] = m_ref[0, :, 0].reshape(128, 128)
    for J in range(8):
        j0 = 128 * J
        r0 = j0 + 128
        r1 = r0 + 128
        S = [B[pl.ds(j0 + 8 * g, 8), :] for g in range(16)]
        U, V = factor(S, E0, scr, lambda: middle(J))
        after(J)
        if J < 7:
            value = m_ref[J + 1:, :, J + 1].reshape(1024 - r0, 128)
            if J > 0:
                value = value - dt(L[pl.ds(r0, 1024 - r0), pl.ds(0, j0)], L[pl.ds(r0, 128), pl.ds(0, j0)])
            T[pl.ds(r0, 1024 - r0), :] = value
        for K in FURTHER[J]:
            further(K)
        if J == 7:
            T[pl.ds(0, 192), :] = tile_ref[1:].reshape(192, 128) - dt(
                L[pl.ds(1024, 192), pl.ds(0, 896)], L[pl.ds(1216, 128), pl.ds(0, 896)])
        Um = jnp.concatenate([jnp.where(lane >= sub + 8 * g, U[g], 0.0) for g in range(16)], 0)
        Vm = jnp.concatenate(V, 0)
        Vs[J] = Vm
        L[pl.ds(j0, 128), pl.ds(j0, 128)] = Um.T
        if J < 7:
            Pn = dt(B[pl.ds(r0, 128), :], Vm)
            L[pl.ds(r0, 128), pl.ds(j0, 128)] = Pn
            B[pl.ds(r0, 128), :] = T[pl.ds(r0, 128), :] - dt(Pn, Pn)
        if J < 6:
            Pr = dt(B[pl.ds(r1, 1024 - r1), :], Vm)
            L[pl.ds(r1, 1024 - r1), pl.ds(j0, 128)] = Pr
            B[pl.ds(r1, 1024 - r1), :] = T[pl.ds(r1, 1024 - r1), :] - dt(Pr, Pn)
    further(7)
    tr = T[pl.ds(0, 192), :] - dt(L[pl.ds(1024, 192), pl.ds(896, 128)], L[pl.ds(1216, 128), pl.ds(896, 128)])
    column = pl.multiple_of(jnp.minimum(c, 7) * 128, 128)
    top = L[pl.ds(pl.multiple_of(r * 64, 64), 64), pl.ds(column, 128)]
    solved = L[pl.ds(1024, 192), pl.ds(column, 128)]
    in_panel = c < 8
    below = lax.broadcasted_iota(jnp.int32, (64, 128), 1) + column <= lax.broadcasted_iota(jnp.int32, (64, 128), 0) + r * 64
    out_ref[0] = jnp.where(jnp.logical_and(in_panel, below), top, 0.0)
    out_ref[1:] = jnp.where(in_panel, solved, tr).reshape(3, 64, 128)

    top_sends(lambda copy: copy.wait_send())
    for group in range(len(GROUPS)):
        row_sends(group, lambda copy: copy.wait_send())
        core_copy(group).wait_send()
    for way in range(2):
        for step in range(1, steps[way] + 1):
            for chunk in range(CHUNKS):
                ring_copy(way, step, chunk).wait_send()
    for copy in near_copies + band_copies:
        copy.wait_send()

    @pl.when(source0)
    def _():
        for copy in lead + second:
            copy.wait_send()

    @pl.when(source1)
    def _():
        for copy in third:
            copy.wait_send()

    pltpu.make_async_copy(prod.at[pl.ds(0, 7)], prod.at[pl.ds(0, 7)], part_send).wait()
    pltpu.make_async_copy(prod.at[pl.ds(0, 8)], prod.at[pl.ds(0, 8)], sib_send).wait()


def body(interactions, regular):
    vmem = pl.BlockSpec(memory_space=pltpu.VMEM)
    dma = pltpu.SemaphoreType.DMA
    rows = 1024 + 192 + 128
    return pl.pallas_call(
        whole_kernel,
        out_shape=jax.ShapeDtypeStruct((4, 64, 128), jnp.float32),
        in_specs=[vmem, vmem],
        out_specs=vmem,
        scratch_shapes=[
            pltpu.VMEM((4, 64, 128), jnp.float32),
            pltpu.VMEM((8, 2, 9, 64, 128), jnp.float32),
            pltpu.VMEM((8, 3, 64, 128), jnp.float32),
            pltpu.VMEM((rows, PANEL), jnp.float32),
            pltpu.VMEM((rows, 128), jnp.float32),
            pltpu.VMEM((rows, 128), jnp.float32),
            pltpu.VMEM((8, 128, 128), jnp.float32),
            pltpu.VMEM((16, 10, 8, 128), jnp.float32),
            pltpu.VMEM((RING, 128, 512), jnp.bfloat16),
            pltpu.VMEM((2, 128, 512), jnp.bfloat16),
            pltpu.VMEM((512, 256), jnp.bfloat16),
            pltpu.VMEM((RING, 2, 64, 256), jnp.float32),
            pltpu.VMEM((RING, 64, 256), jnp.float32),
            pltpu.VMEM((2, 8, 64, 256), jnp.float32),
            pltpu.VMEM((2, 2, 64, 128), jnp.float32),
            dma((2, 8, CHUNKS)),
            dma((2, 8, CHUNKS)),
            dma((2,)),
            dma((2,)),
            dma,
            dma((16,)),
            dma,
            dma((2,)),
            dma((3, 3)),
            dma((3,)),
            dma((2, 7)),
            dma((2, 7)),
            dma((15,)),
            dma((2,)),
            dma((len(GROUPS), 7)),
            dma((len(GROUPS),)),
            dma((len(GROUPS),)),
            dma((len(GROUPS),)),
        ],
        compiler_params=pltpu.CompilerParams(
            collective_id=0, has_side_effects=True, vmem_limit_bytes=50 * 1024 * 1024
        ),
        name="whole",
    )(interactions, regular.reshape(1, 128))


def solution(mesh):
    return jax.shard_map(
        body,
        mesh=mesh,
        in_specs=(P("col", "row"), P("col")),
        out_specs=P(None, "row", "col"),
        check_vma=False,
    )
```
